32 devices in a mesh: tm: 8 (over z, core), cell: 4 (over y, x).
Axes of the slice: x: 2, y: 2, z: 4, core: 2. Of those that a mesh axis runs over, the one named last changes fastest.
Arguments:
- points: float32 [8, 30, 2048], P('tm', None, 'cell')
- last_points: float32 [30, 2048], P(None, 'cell'), may hold values from -5 to 5
- counts: int32 [9], replicated, may hold values from 512 to 2048
- bins: int32 [8, 2048], P('tm', 'cell'), may hold values from 0 to 15
- rates: float32 [8, 16], P('tm'), may hold values from 0.25 to 4
Outputs:
- source_potential: float32 [8, 2048], P('tm', 'cell')
- target_potential: float32 [8, 2048], P('tm', 'cell')
- ancestor_mass: float32 [8, 2048], P('tm', 'cell')
The draws below stay inside these ranges and needn't reach their ends.
All inputs are finite; a program needn't handle non-finite values.
Results may differ from the reference program's by a relative error of at most 0.0003.
Values sent between devices are 32-bit elements; how exact they have to be, the bound alone decides.
A program may use at most 64 MiB of HBM per device.

```python
import math
import jax
import jax.numpy as jnp
from jax import lax

PC = 30
NBINS = 16
ITERS = 4
CELLS = 2048
NT = 8


def draw_points(key, part):
    key = jax.random.fold_in(key, 1)
    base = jnp.clip(jax.random.normal(key, (NT, PC, CELLS), jnp.float32), -5.0, 5.0)
    signs = jax.random.randint(jax.random.fold_in(key, 3), (NT, PC, 2), 0, 2).astype(jnp.float32) * 2.0 - 1.0
    strength = jnp.array([14.0, 30.0], jnp.float32)
    offset = signs * jnp.sqrt(strength * 60.0 / PC)[None, None, :]
    base = base.at[:, :, 0:2].add(offset)
    return base


def set_ends(result, rng, low, high):
    extent = result.shape
    spot = [jax.random.randint(jax.random.fold_in(rng, axis), (), 0, extent[axis]) for axis in range(len(extent))]
    result = result.at[tuple(spot)].set(low)
    longest = extent.index(max(extent))
    spot[longest] = (spot[longest] + 1) % extent[longest]
    return result.at[tuple(spot)].set(high)


def shard_levels(own_key, dims, shards, smallest, high):
    gain, own = 1.0, jax.random.fold_in(own_key, 6)
    for position, shards_of in shards:
        steps = jnp.exp(jax.random.uniform(jax.random.fold_in(own, position), (shards_of,), jnp.float32, smallest / len(shards), high / len(shards)))
        gain = gain * jnp.repeat(steps, dims[position] // shards_of).reshape([-1 if axis == position else 1 for axis in range(len(dims))])
    return gain


def bell_draw(rng, shape, scale, most, pieces=(), kind=jnp.bfloat16):
    result = jax.random.normal(rng, shape, jnp.float32) * scale
    if len(pieces) > 0:
        result = shard_levels(rng, shape, pieces, -0.22, 0.18) * result
    return jnp.clip(result, min=-most, max=most).astype(kind)


def setup_inputs(seed: int = 0) -> dict:
    key_of = jax.random.split(jax.random.key(seed), 6)
    return {
        "points": draw_points(jax.random.fold_in(key_of[5], 71), 0),
        "last_points": bell_draw(key_of[1], (PC, CELLS), 1.0, 5.0, ((1, 4),), jnp.float32),
        "counts": set_ends(jax.random.randint(key_of[2], (NT + 1,), CELLS // 4, CELLS + 1), jax.random.fold_in(key_of[2], 1), CELLS // 4, CELLS).astype(jnp.int32),
        "bins": set_ends(jax.random.randint(key_of[3], (NT, CELLS), 0, NBINS), jax.random.fold_in(key_of[3], 1), 0, NBINS - 1).astype(jnp.int32),
        "rates": jnp.clip(jnp.exp(math.log(4.0) - 2.7725887 * jax.random.uniform(key_of[4], (NT, NBINS), jnp.float32) ** shard_levels(key_of[4], (NT, NBINS), ((0, 8),), -0.2, 0.2)), 0.25, 4.0),
    }


EPS = 0.05
FI = 1.0 / 1.05
FJ = 50.0 / 50.05
NEG = -1e30


def lse_rows(score):
    top = jnp.max(score, axis=1)
    return top + jnp.log(jnp.sum(jnp.exp(score - top[:, None]), axis=1))


def lse_cols(score):
    top = jnp.max(score, axis=0)
    return top + jnp.log(jnp.sum(jnp.exp(score - top[None, :]), axis=0))


def one_pair(source, target, nsrc, ntgt, bin_row, rate_row):
    index = jnp.arange(CELLS, dtype=jnp.int32)
    live_s = index < nsrc
    live_t = index < ntgt
    sqx = jnp.sum(source * source, axis=0)
    sqy = jnp.sum(target * target, axis=0)
    cross = jnp.dot(source.T, target, precision=lax.Precision.HIGHEST)
    cost = sqx[:, None] + sqy[None, :] - 2.0 * cross
    both = live_s[:, None] & live_t[None, :]
    cbar = jnp.sum(jnp.where(both, cost, 0.0)) / (nsrc.astype(jnp.float32) * ntgt.astype(jnp.float32))
    scaled = cost / cbar
    table = bin_row[None, :] == jnp.arange(NBINS, dtype=jnp.int32)[:, None]
    growth = jnp.sum(jnp.where(table, rate_row[:, None], 0.0), axis=0)
    gbar = jnp.sum(jnp.where(live_s, growth, 0.0)) / nsrc.astype(jnp.float32)
    loga = jnp.log(growth) - jnp.log(gbar)
    fpot = jnp.zeros((CELLS,), jnp.float32)
    hpot = jnp.zeros((CELLS,), jnp.float32)
    zero_rows = jnp.zeros((CELLS,), jnp.float32)
    for step in range(ITERS):
        score = jnp.where(live_t[None, :], (zero_rows[:, None] + hpot[None, :] - scaled) / EPS, NEG)
        fpot = jnp.where(live_s, FI * (EPS * loga - EPS * lse_rows(score)), 0.0)
        score = jnp.where(live_s[:, None], (fpot[:, None] - scaled) / EPS, NEG)
        hpot = jnp.where(live_t, FJ * (-EPS * lse_cols(score)), 0.0)
    score = jnp.where(live_t[None, :], (fpot[:, None] + hpot[None, :] - scaled) / EPS, NEG)
    mass = jnp.where(live_s, jnp.exp(lse_rows(score)), 0.0)
    return fpot, hpot, mass


def reference(points, last_points, counts, bins, rates):
    targets = jnp.concatenate([points[1:], last_points[None]], axis=0)

    def step(item):
        source, target, nsrc, ntgt, bin_row, rate_row = item
        return one_pair(source, target, nsrc, ntgt, bin_row, rate_row)

    fpot, hpot, mass = lax.map(step, (points, targets, counts[:-1], counts[1:], bins, rates))
    return fpot, hpot, mass
```

```python
import functools
import math

import jax
import jax.numpy as jnp
from jax import lax
from jax.experimental import pallas as pl
from jax.experimental.pallas import tpu as pltpu
from jax.sharding import PartitionSpec as P

ITERS = 4

EPS = 0.05
FI = 1.0 / 1.05
FJ = 50.0 / 50.05
NEG = -1e30
LOG2E = math.log2(math.e)
UNIT = LOG2E / EPS

LANE = 128
SUB = 8
MESH = pl.DeviceIdType.MESH


def each(count, body):
    if count <= 4:
        for item in range(count):
            body(item)
    else:
        pl.loop(0, count)(body)


def tree(join, parts):
    while len(parts) > 1:
        parts = [join(*parts[i : i + 2]) if i + 1 < len(parts) else parts[i] for i in range(0, len(parts), 2)]
    return parts[0]


def splits(value):
    first = value.astype(jnp.bfloat16)
    rest = value - first.astype(jnp.float32)
    second = rest.astype(jnp.bfloat16)
    third = (rest - second.astype(jnp.float32)).astype(jnp.bfloat16)
    return first, second, third


def lane_totals(rows):
    part = tree(jnp.add, [rows[:, i : i + LANE] for i in range(0, rows.shape[1], LANE)])
    whole = jnp.concatenate([part, jnp.zeros((LANE - part.shape[0], LANE), jnp.float32)], axis=0)
    return jnp.sum(whole.T, axis=0, keepdims=True)


def kernel(nt, nc, points, last, counts, bins, rates, fout, hout, mout,
           cost, tgt, stats, parts, lhs, pot, row_max, row_sum, level, colpot,
           tgt_send, last_send, tgt_recv, st_send, st_recv, p_send, p_recv):
    t = lax.axis_index("tm")
    c = lax.axis_index("cell")
    pc, n = tgt.shape[1:]
    cells = nc * n
    tiles = n // SUB
    blocks = cells // LANE
    f32 = jnp.float32

    barrier = pltpu.get_barrier_semaphore()

    def peer(step):
        return lax.rem(c + step, nc)

    @pl.when(t < nt - 1)
    def _():
        for k in range(nc):
            pl.semaphore_signal(barrier, inc=1, device_id={"tm": t + 1, "cell": k}, device_id_type=MESH)

    for step in range(1, nc):
        pl.semaphore_signal(barrier, inc=1, device_id={"tm": t, "cell": peer(step)}, device_id_type=MESH)

    nsrc = counts[t]
    ntgt = counts[t + 1]
    mine = nsrc - c * n
    live = lax.broadcasted_iota(jnp.int32, (1, n), 1) < mine
    x = jnp.where(live, points[0], 0.0)
    sqx = jnp.sum(x * x, axis=0, keepdims=True)
    growth = jnp.zeros((1, n), f32)
    for k in range(rates.shape[1]):
        growth = jnp.where(bins[...] == k, rates[0, k], growth)
    stats[c] = lane_totals(jnp.concatenate([x, sqx, jnp.where(live, growth, 0.0)], axis=0))
    x1, x2, x3 = splits(jnp.concatenate([-2.0 * x, sqx, jnp.ones((1, n), f32)], axis=0))
    stacked = jnp.concatenate([x1, x1, x2, x2, x1, x3], axis=0)
    lhs[...] = stacked.T

    @pl.when(t == 0)
    def _():
        pl.semaphore_wait(barrier, nc - 1)

    @pl.when(t > 0)
    def _():
        pl.semaphore_wait(barrier, 2 * nc - 1)

    def stat_copy(step, slot):
        return pltpu.make_async_remote_copy(
            stats.at[slot], stats.at[slot], st_send.at[step], st_recv.at[slot],
            device_id={"tm": t, "cell": peer(step)}, device_id_type=MESH)

    def tgt_copy(step):
        return pltpu.make_async_remote_copy(
            points.at[0], tgt.at[c], tgt_send.at[step], tgt_recv.at[c],
            device_id={"tm": t - 1, "cell": peer(step)}, device_id_type=MESH)

    def last_copy(step):
        return pltpu.make_async_remote_copy(
            last, tgt.at[c], last_send.at[step], tgt_recv.at[c],
            device_id={"tm": t, "cell": peer(step)}, device_id_type=MESH)

    for step in range(1, nc):
        stat_copy(step, c).start()

    @pl.when(t > 0)
    def _():
        for step in range(nc):
            tgt_copy(step).start()

    @pl.when(t == nt - 1)
    def _():
        for step in range(1, nc):
            last_copy(step).start()
        pltpu.make_async_copy(last, tgt.at[c], tgt_recv.at[c]).start()

    for step in range(1, nc):
        stat_copy(step, peer(step)).wait_recv()
    source = tree(jnp.add, [stats[k] for k in range(nc)])
    lane = lax.broadcasted_iota(jnp.int32, (1, LANE), 1)

    def pick(row, index):
        return jnp.sum(jnp.where(lane == index, row, 0.0), axis=1, keepdims=True)

    nsrc_f = nsrc.astype(f32)
    ntgt_f = ntgt.astype(f32)
    gbar = pick(source, pc + 1) / nsrc_f
    loga = (jnp.log(growth) - jnp.log(gbar)) * LOG2E
    for k in range(n // LANE):
        wide = jnp.broadcast_to(loga[:, k * LANE : (k + 1) * LANE], (LANE, LANE))
        level[k * (LANE // SUB) : (k + 1) * (LANE // SUB)] = wide.T.reshape(LANE // SUB, SUB, LANE)

    colpot[...] = jnp.zeros_like(colpot)
    stats[nc] = jnp.zeros((1, LANE), f32)

    def take(step):
        k = peer(step)
        pltpu.make_async_copy(tgt.at[k], tgt.at[k], tgt_recv.at[k]).wait()
        ok = lax.broadcasted_iota(jnp.int32, (1, n), 1) < ntgt - k * n
        y = jnp.where(ok, tgt[k], 0.0)
        sqy = jnp.sum(y * y, axis=0, keepdims=True)
        one = jnp.ones((1, n), f32)
        stats[nc] += lane_totals(jnp.concatenate([y, sqy, jnp.zeros((1, n), f32)], axis=0))
        y1, y2, y3 = splits(jnp.concatenate([y, one, sqy], axis=0))
        rhs = jnp.concatenate([y1, y2, y1, y2, y3, y1], axis=0)
        cols = pl.ds(pl.multiple_of(k * n, LANE), n)
        for rb in range(n // LANE):
            got = jnp.dot(lhs[rb * LANE : (rb + 1) * LANE], rhs, preferred_element_type=f32)
            cost[rb * (LANE // SUB) : (rb + 1) * (LANE // SUB), :, cols] = got.reshape(LANE // SUB, SUB, n)
        dead = jnp.where(ok, 0.0, NEG)
        for b in range(n // LANE):
            colpot[k * (n // LANE) + b] = jnp.broadcast_to(dead[:, b * LANE : (b + 1) * LANE], (SUB, LANE))

    each(nc, take)
    target = stats[nc]
    both = jnp.sum(jnp.where(lane < pc, source * target, 0.0), axis=1, keepdims=True)
    total = ntgt_f * pick(source, pc) + nsrc_f * pick(target, pc) - 2.0 * both
    cbar = total / (nsrc_f * ntgt_f)
    scale = jnp.broadcast_to(-UNIT / cbar, (SUB, LANE))
    sub_row = lax.broadcasted_iota(jnp.int32, (SUB, LANE), 0)

    def rows_pass(first):
        @pl.loop(0, tiles // 4)
        def _(i):
            for u in range(4):
                r = i * 4 + u
                scores = []
                for j in range(blocks):
                    piece = cost[r, :, j * LANE : (j + 1) * LANE]
                    if first:
                        piece = piece * scale
                        cost[r, :, j * LANE : (j + 1) * LANE] = piece
                    scores.append(piece + colpot[j])
                top = tree(jnp.maximum, scores)
                row_max[r] = top
                row_sum[r] = tree(jnp.add, [jnp.exp2(s - top) for s in scores])

    def rows_lse(r):
        top = jnp.max(row_max[r], axis=1, keepdims=True)
        add = jnp.sum(row_sum[r] * jnp.exp2(row_max[r] - top), axis=1, keepdims=True)
        return top + jnp.log(add) * LOG2E

    def rows_end():
        @pl.loop(0, tiles // 16)
        def _(i):
            for u in range(16):
                r = i * 16 + u
                fpot = FI * (level[r] - rows_lse(r))
                pot[r] = jnp.where(sub_row + r * SUB < mine, fpot, NEG)

    def cols_pass(it):
        @pl.loop(0, blocks // 2)
        def _(i):
            for b in range(2):
                j = i * 2 + b
                cols = pl.ds(pl.multiple_of(j * LANE, LANE), LANE)
                tops = [None] * 4
                for r in range(tiles):
                    s = pot[r] + cost[r, :, cols]
                    tops[r % 4] = s if r < 4 else jnp.maximum(tops[r % 4], s)
                top = tree(jnp.maximum, tops)
                sums = [None] * 4
                for r in range(tiles):
                    e = jnp.exp2(pot[r] + cost[r, :, cols] - top)
                    sums[r % 4] = e if r < 4 else sums[r % 4] + e
                add = tree(jnp.add, sums)
                most = jnp.max(top, axis=0, keepdims=True)
                add = jnp.sum(add * jnp.exp2(top - most), axis=0, keepdims=True)
                parts[it, c, pl.ds(j, 1)] = most + jnp.log(add) * LOG2E

    def part_copy(it, step, slot):
        return pltpu.make_async_remote_copy(
            parts.at[it, slot], parts.at[it, slot], p_send.at[it, step], p_recv.at[it, slot],
            device_id={"tm": t, "cell": peer(step)}, device_id_type=MESH)

    cell_at = (lax.broadcasted_iota(jnp.int32, (blocks, LANE), 0) * LANE
               + lax.broadcasted_iota(jnp.int32, (blocks, LANE), 1))

    def exchange(it):
        for step in range(1, nc):
            part_copy(it, step, c).start()
        for step in range(1, nc):
            part_copy(it, step, peer(step)).wait_recv()
        pieces = [parts[it, k] for k in range(nc)]
        top = tree(jnp.maximum, pieces)
        add = tree(jnp.add, [jnp.exp2(p - top) for p in pieces])
        hpot = jnp.where(cell_at < ntgt, -FJ * (top + jnp.log(add) * LOG2E), NEG)
        for j in range(blocks):
            colpot[j] = jnp.broadcast_to(hpot[j : j + 1], (SUB, LANE))

    def one(it, first):
        rows_pass(first)
        rows_end()
        cols_pass(it)
        exchange(it)

    one(0, True)

    @pl.loop(1, ITERS)
    def _(it):
        one(it, False)

    rows_pass(False)
    per = LANE // SUB
    for k in range(n // LANE):
        fpot = pot[k * per : (k + 1) * per].reshape(LANE, LANE)
        ok = lax.broadcasted_iota(jnp.int32, (LANE, LANE), 0) + k * LANE < mine
        lse = jnp.concatenate([jnp.broadcast_to(rows_lse(k * per + r), (SUB, LANE)) for r in range(per)], axis=0)
        mass = jnp.where(ok, jnp.exp2(fpot + lse), 0.0)
        fout[:, k * LANE : (k + 1) * LANE] = jnp.where(ok, fpot * (1.0 / UNIT), 0.0).T[0:1]
        mout[:, k * LANE : (k + 1) * LANE] = mass.T[0:1]
        j = c * (n // LANE) + k
        own = colpot[j][0:1]
        good = lane + j * LANE < ntgt
        hout[:, k * LANE : (k + 1) * LANE] = jnp.where(good, own * (1.0 / UNIT), 0.0)

    for step in range(1, nc):
        stat_copy(step, c).wait_send()
        for it in range(ITERS):
            part_copy(it, step, c).wait_send()

    @pl.when(t > 0)
    def _():
        for step in range(nc):
            tgt_copy(step).wait_send()

    @pl.when(t == nt - 1)
    def _():
        for step in range(1, nc):
            last_copy(step).wait_send()


def local(points, last_points, counts, bins, rates):
    nt = lax.axis_size("tm")
    nc = lax.axis_size("cell")
    pc, n = last_points.shape
    cells = nc * n
    f32 = jnp.float32
    vmem = pl.BlockSpec(memory_space=pltpu.VMEM)
    smem = pl.BlockSpec(memory_space=pltpu.SMEM)
    row = jax.ShapeDtypeStruct((1, n), f32)
    tile = pltpu.VMEM((n // SUB, SUB, LANE), f32)
    dma = pltpu.SemaphoreType.DMA
    return pl.pallas_call(
        functools.partial(kernel, nt, nc),
        out_shape=(row, row, row),
        in_specs=[vmem, vmem, smem, vmem, smem],
        out_specs=(vmem, vmem, vmem),
        scratch_shapes=[
            pltpu.VMEM((n // SUB, SUB, cells), f32),
            pltpu.VMEM((nc, pc, n), f32),
            pltpu.VMEM((nc + 1, 1, LANE), f32),
            pltpu.VMEM((ITERS, nc, cells // LANE, LANE), f32),
            pltpu.VMEM((n, 6 * (pc + 2)), jnp.bfloat16),
            tile, tile, tile, tile,
            pltpu.VMEM((cells // LANE, SUB, LANE), f32),
            dma((nc,)), dma((nc,)), dma((nc,)), dma((nc,)), dma((nc,)),
            dma((ITERS, nc)), dma((ITERS, nc)),
        ],
        compiler_params=pltpu.CompilerParams(
            collective_id=0, has_side_effects=True, vmem_limit_bytes=48 * 1024 * 1024
        ),
        name="coupling",
    )(points, last_points, counts, bins, rates)


def solution(mesh):
    return jax.shard_map(
        local,
        mesh=mesh,
        in_specs=(P("tm", None, "cell"), P(None, "cell"), P(), P("tm", "cell"), P("tm", None)),
        out_specs=(P("tm", "cell"), P("tm", "cell"), P("tm", "cell")),
        check_vma=False,
    )
```

```python
import functools
import math

import jax
import jax.numpy as jnp
from jax import lax
from jax.experimental import pallas as pl
from jax.experimental.pallas import tpu as pltpu
from jax.sharding import PartitionSpec as P

ITERS = 4

EPS = 0.05
FI = 1.0 / 1.05
FJ = 50.0 / 50.05
NEG = -1e30
LOG2E = math.log2(math.e)
UNIT = LOG2E / EPS

LANE = 128
HALVES = 2
GROUP = 8
WIDE = 4
SUB = 8
MESH = pl.DeviceIdType.MESH


def each(count, body):
    if count <= 4:
        for item in range(count):
            body(item)
    else:
        pl.loop(0, count)(body)


def tree(join, parts):
    while len(parts) > 1:
        parts = [join(*parts[i : i + 2]) if i + 1 < len(parts) else parts[i] for i in range(0, len(parts), 2)]
    return parts[0]


def splits(value):
    first = value.astype(jnp.bfloat16)
    rest = value - first.astype(jnp.float32)
    second = rest.astype(jnp.bfloat16)
    third = (rest - second.astype(jnp.float32)).astype(jnp.bfloat16)
    return first, second, third


def lane_totals(rows):
    part = tree(jnp.add, [rows[:, i : i + LANE] for i in range(0, rows.shape[1], LANE)])
    whole = jnp.concatenate([part, jnp.zeros((LANE - part.shape[0], LANE), jnp.float32)], axis=0)
    return jnp.sum(whole.T, axis=0, keepdims=True)


def kernel(nt, nc, points, last, counts, bins, rates, fout, hout, mout,
           cost, tgt, stats, parts, lhs, pot, row_max, row_sum, level, colpot,
           tgt_send, last_send, tgt_recv, st_send, st_recv, p_send, p_recv):
    t = lax.axis_index("tm")
    c = lax.axis_index("cell")
    pc, n = tgt.shape[1:]
    cells = nc * n
    tiles = n // SUB
    blocks = cells // LANE
    f32 = jnp.float32

    barrier = pltpu.get_barrier_semaphore()

    def peer(step):
        return lax.rem(c + step, nc)

    @pl.when(t < nt - 1)
    def _():
        for k in range(nc):
            pl.semaphore_signal(barrier, inc=1, device_id={"tm": t + 1, "cell": k}, device_id_type=MESH)

    for step in range(1, nc):
        pl.semaphore_signal(barrier, inc=1, device_id={"tm": t, "cell": peer(step)}, device_id_type=MESH)

    nsrc = counts[t]
    ntgt = counts[t + 1]
    mine = nsrc - c * n
    live = lax.broadcasted_iota(jnp.int32, (1, n), 1) < mine
    x = jnp.where(live, points[0], 0.0)
    sqx = jnp.sum(x * x, axis=0, keepdims=True)
    growth = jnp.zeros((1, n), f32)
    for k in range(rates.shape[1]):
        growth = jnp.where(bins[...] == k, rates[0, k], growth)
    stats[c] = lane_totals(jnp.concatenate([x, sqx, jnp.where(live, growth, 0.0)], axis=0))
    x1, x2, x3 = splits(jnp.concatenate([-2.0 * x, sqx, jnp.ones((1, n), f32)], axis=0))
    stacked = jnp.concatenate([x1, x1, x2, x2, x1, x3], axis=0)
    lhs[...] = stacked.T

    @pl.when(t == 0)
    def _():
        pl.semaphore_wait(barrier, nc - 1)

    @pl.when(t > 0)
    def _():
        pl.semaphore_wait(barrier, 2 * nc - 1)

    def stat_copy(step, slot):
        return pltpu.make_async_remote_copy(
            stats.at[slot], stats.at[slot], st_send.at[step], st_recv.at[slot],
            device_id={"tm": t, "cell": peer(step)}, device_id_type=MESH)

    def tgt_copy(step):
        return pltpu.make_async_remote_copy(
            points.at[0], tgt.at[c], tgt_send.at[step], tgt_recv.at[c],
            device_id={"tm": t - 1, "cell": peer(step)}, device_id_type=MESH)

    def last_copy(step):
        return pltpu.make_async_remote_copy(
            last, tgt.at[c], last_send.at[step], tgt_recv.at[c],
            device_id={"tm": t, "cell": peer(step)}, device_id_type=MESH)

    for step in range(1, nc):
        stat_copy(step, c).start()

    @pl.when(t > 0)
    def _():
        for step in range(nc):
            tgt_copy(step).start()

    @pl.when(t == nt - 1)
    def _():
        for step in range(1, nc):
            last_copy(step).start()
        pltpu.make_async_copy(last, tgt.at[c], tgt_recv.at[c]).start()

    for step in range(1, nc):
        stat_copy(step, peer(step)).wait_recv()
    source = tree(jnp.add, [stats[k] for k in range(nc)])
    lane = lax.broadcasted_iota(jnp.int32, (1, LANE), 1)

    def pick(row, index):
        return jnp.sum(jnp.where(lane == index, row, 0.0), axis=1, keepdims=True)

    nsrc_f = nsrc.astype(f32)
    ntgt_f = ntgt.astype(f32)
    gbar = pick(source, pc + 1) / nsrc_f
    loga = (jnp.log(growth) - jnp.log(gbar)) * LOG2E
    for k in range(n // LANE):
        wide = jnp.broadcast_to(loga[:, k * LANE : (k + 1) * LANE], (LANE, LANE))
        level[k * (LANE // SUB) : (k + 1) * (LANE // SUB)] = wide.T.reshape(LANE // SUB, SUB, LANE)

    colpot[...] = jnp.zeros_like(colpot)
    stats[nc] = jnp.zeros((1, LANE), f32)

    def take(step):
        k = peer(step)
        pltpu.make_async_copy(tgt.at[k], tgt.at[k], tgt_recv.at[k]).wait()
        ok = lax.broadcasted_iota(jnp.int32, (1, n), 1) < ntgt - k * n
        y = jnp.where(ok, tgt[k], 0.0)
        sqy = jnp.sum(y * y, axis=0, keepdims=True)
        one = jnp.ones((1, n), f32)
        stats[nc] += lane_totals(jnp.concatenate([y, sqy, jnp.zeros((1, n), f32)], axis=0))
        y1, y2, y3 = splits(jnp.concatenate([y, one, sqy], axis=0))
        rhs = jnp.concatenate([y1, y2, y1, y2, y3, y1], axis=0)
        cols = pl.ds(pl.multiple_of(k * n, LANE), n)
        for rb in range(n // LANE):
            got = jnp.dot(lhs[rb * LANE : (rb + 1) * LANE], rhs, preferred_element_type=f32)
            cost[rb * (LANE // SUB) : (rb + 1) * (LANE // SUB), :, cols] = got.reshape(LANE // SUB, SUB, n)
        dead = jnp.where(ok, 0.0, NEG)
        for b in range(n // LANE):
            colpot[k * (n // LANE) + b] = jnp.broadcast_to(dead[:, b * LANE : (b + 1) * LANE], (SUB, LANE))

    each(nc, take)
    target = stats[nc]
    both = jnp.sum(jnp.where(lane < pc, source * target, 0.0), axis=1, keepdims=True)
    total = ntgt_f * pick(source, pc) + nsrc_f * pick(target, pc) - 2.0 * both
    cbar = total / (nsrc_f * ntgt_f)
    scale = jnp.broadcast_to(-UNIT / cbar, (SUB, LANE))
    sub_row = lax.broadcasted_iota(jnp.int32, (SUB, LANE), 0)

    half = blocks // HALVES

    def rows_part(r, h, first):
        scores = []
        for j in range(h * half, (h + 1) * half):
            piece = cost[r, :, j * LANE : (j + 1) * LANE]
            if first:
                piece = piece * scale
                cost[r, :, j * LANE : (j + 1) * LANE] = piece
            scores.append(piece + colpot[j])
        top = tree(jnp.maximum, scores)
        if h > 0:
            before = row_max[r]
            top = jnp.maximum(top, before)
        add = tree(jnp.add, [jnp.exp2(s - top) for s in scores])
        if h > 0:
            add += row_sum[r] * jnp.exp2(before - top)
        row_max[r] = top
        row_sum[r] = add

    def rows_end(r, final):
        top = jnp.max(row_max[r], axis=1, keepdims=True)
        add = jnp.sum(row_sum[r] * jnp.exp2(row_max[r] - top), axis=1, keepdims=True)
        lse = top + jnp.log(add) * LOG2E
        if final:
            level[r] = jnp.exp2(pot[r] + lse)
        else:
            pot[r] = jnp.where(sub_row + r * SUB < mine, FI * (level[r] - lse), NEG)

    def rows_open(h, first):
        @pl.loop(0, tiles // GROUP)
        def _(i):
            for u in range(GROUP):
                rows_part(i * GROUP + u, h, first)

    def rows_close(h, first, final):
        for u in range(GROUP):
            rows_part(u, h, first)

        @pl.loop(1, tiles // GROUP)
        def _(i):
            for u in range(GROUP):
                rows_end((i - 1) * GROUP + u, final)
            for u in range(GROUP):
                rows_part(i * GROUP + u, h, first)

        for u in range(GROUP):
            rows_end(tiles - GROUP + u, final)

    def cols_part(it, h):
        @pl.loop(0, half // WIDE)
        def _(i):
            at = [pl.multiple_of((h * half + i * WIDE + b) * LANE, LANE) for b in range(WIDE)]
            tops = [[None, None] for _ in at]
            for r in range(tiles):
                base = pot[r]
                for b in range(WIDE):
                    s = base + cost[r, :, pl.ds(at[b], LANE)]
                    tops[b][r % 2] = s if r < 2 else jnp.maximum(tops[b][r % 2], s)
            top = [jnp.maximum(*pair) for pair in tops]
            sums = [[None, None] for _ in at]
            for r in range(tiles):
                base = pot[r]
                for b in range(WIDE):
                    e = jnp.exp2(base + cost[r, :, pl.ds(at[b], LANE)] - top[b])
                    sums[b][r % 2] = e if r < 2 else sums[b][r % 2] + e
            for b in range(WIDE):
                most = jnp.max(top[b], axis=0, keepdims=True)
                add = (sums[b][0] + sums[b][1]) * jnp.exp2(top[b] - most)
                lse = most + jnp.log(jnp.sum(add, axis=0, keepdims=True)) * LOG2E
                parts[it, c, h, pl.ds(i * WIDE + b, 1)] = lse

    def part_copy(it, step, slot, h):
        return pltpu.make_async_remote_copy(
            parts.at[it, slot, h], parts.at[it, slot, h], p_send.at[it, step, h], p_recv.at[it, slot, h],
            device_id={"tm": t, "cell": peer(step)}, device_id_type=MESH)

    cell_at = (lax.broadcasted_iota(jnp.int32, (half, LANE), 0) * LANE
               + lax.broadcasted_iota(jnp.int32, (half, LANE), 1))

    def joined(it, h):
        for step in range(1, nc):
            part_copy(it, step, peer(step), h).wait_recv()
        pieces = [parts[it, k, h] for k in range(nc)]
        top = tree(jnp.maximum, pieces)
        add = tree(jnp.add, [jnp.exp2(p - top) for p in pieces])
        ok = cell_at < ntgt - h * half * LANE
        hpot = jnp.where(ok, -FJ * (top + jnp.log(add) * LOG2E), NEG)
        for j in range(half):
            colpot[h * half + j] = jnp.broadcast_to(hpot[j : j + 1], (SUB, LANE))

    def one(it, final):
        for h in range(HALVES):
            cols_part(it, h)
            for step in range(1, nc):
                part_copy(it, step, c, h).start()
        joined(it, 0)
        rows_open(0, False)
        joined(it, 1)
        rows_close(1, False, final)

    rows_open(0, True)
    rows_close(1, True, False)

    @pl.loop(0, ITERS - 1)
    def _(it):
        one(it, False)

    one(ITERS - 1, True)
    per = LANE // SUB
    for k in range(n // LANE):
        cols = slice(k * LANE, (k + 1) * LANE)
        ok = lane + k * LANE < mine
        fpot = pot[k * per : (k + 1) * per].reshape(LANE, LANE).T[0:1]
        mass = level[k * per : (k + 1) * per].reshape(LANE, LANE).T[0:1]
        fout[:, cols] = jnp.where(ok, fpot * (1.0 / UNIT), 0.0)
        mout[:, cols] = jnp.where(ok, mass, 0.0)
        j = c * (n // LANE) + k
        good = lane + j * LANE < ntgt
        hout[:, cols] = jnp.where(good, colpot[j][0:1] * (1.0 / UNIT), 0.0)

    for step in range(1, nc):
        stat_copy(step, c).wait_send()
        for it in range(ITERS):
            for h in range(HALVES):
                part_copy(it, step, c, h).wait_send()

    @pl.when(t > 0)
    def _():
        for step in range(nc):
            tgt_copy(step).wait_send()

    @pl.when(t == nt - 1)
    def _():
        for step in range(1, nc):
            last_copy(step).wait_send()


def local(points, last_points, counts, bins, rates):
    nt = lax.axis_size("tm")
    nc = lax.axis_size("cell")
    pc, n = last_points.shape
    cells = nc * n
    f32 = jnp.float32
    vmem = pl.BlockSpec(memory_space=pltpu.VMEM)
    smem = pl.BlockSpec(memory_space=pltpu.SMEM)
    row = jax.ShapeDtypeStruct((1, n), f32)
    tile = pltpu.VMEM((n // SUB, SUB, LANE), f32)
    dma = pltpu.SemaphoreType.DMA
    return pl.pallas_call(
        functools.partial(kernel, nt, nc),
        out_shape=(row, row, row),
        in_specs=[vmem, vmem, smem, vmem, smem],
        out_specs=(vmem, vmem, vmem),
        scratch_shapes=[
            pltpu.VMEM((n // SUB, SUB, cells), f32),
            pltpu.VMEM((nc, pc, n), f32),
            pltpu.VMEM((nc + 1, 1, LANE), f32),
            pltpu.VMEM((ITERS, nc, HALVES, cells // LANE // HALVES, LANE), f32),
            pltpu.VMEM((n, 6 * (pc + 2)), jnp.bfloat16),
            tile, tile, tile, tile,
            pltpu.VMEM((cells // LANE, SUB, LANE), f32),
            dma((nc,)), dma((nc,)), dma((nc,)), dma((nc,)), dma((nc,)),
            dma((ITERS, nc, HALVES)), dma((ITERS, nc, HALVES)),
        ],
        compiler_params=pltpu.CompilerParams(
            collective_id=0, has_side_effects=True, vmem_limit_bytes=48 * 1024 * 1024
        ),
        name="coupling",
    )(points, last_points, counts, bins, rates)


def solution(mesh):
    return jax.shard_map(
        local,
        mesh=mesh,
        in_specs=(P("tm", None, "cell"), P(None, "cell"), P(), P("tm", "cell"), P("tm", None)),
        out_specs=(P("tm", "cell"), P("tm", "cell"), P("tm", "cell")),
        check_vma=False,
    )
```

```python
import functools
import math

import jax
import jax.numpy as jnp
from jax import lax
from jax.experimental import pallas as pl
from jax.experimental.pallas import tpu as pltpu
from jax.sharding import PartitionSpec as P

ITERS = 4

EPS = 0.05
FI = 1.0 / 1.05
FJ = 50.0 / 50.05
NEG = -1e30
LOG2E = math.log2(math.e)
UNIT = LOG2E / EPS

LANE = 128
HALVES = 2
GROUP = 16
WIDE = 4
SUB = 8
MESH = pl.DeviceIdType.MESH


def each(count, body):
    if count <= 4:
        for item in range(count):
            body(item)
    else:
        pl.loop(0, count)(body)


def tree(join, parts):
    while len(parts) > 1:
        parts = [join(*parts[i : i + 2]) if i + 1 < len(parts) else parts[i] for i in range(0, len(parts), 2)]
    return parts[0]


def splits(value):
    first = value.astype(jnp.bfloat16)
    rest = value - first.astype(jnp.float32)
    second = rest.astype(jnp.bfloat16)
    third = (rest - second.astype(jnp.float32)).astype(jnp.bfloat16)
    return first, second, third


def lane_totals(rows):
    part = tree(jnp.add, [rows[:, i : i + LANE] for i in range(0, rows.shape[1], LANE)])
    whole = jnp.concatenate([part, jnp.zeros((LANE - part.shape[0], LANE), jnp.float32)], axis=0)
    return jnp.sum(whole.T, axis=0, keepdims=True)


def kernel(nt, nc, points, last, counts, bins, rates, fout, hout, mout,
           cost, tgt, stats, parts, lhs, pot, row_max, row_sum, level, fpot, colpot,
           tgt_send, last_send, tgt_recv, st_send, st_recv, p_send, p_recv):
    t = lax.axis_index("tm")
    c = lax.axis_index("cell")
    pc, n = tgt.shape[1:]
    cells = nc * n
    tiles = n // SUB
    blocks = cells // LANE
    f32 = jnp.float32

    barrier = pltpu.get_barrier_semaphore()

    def peer(step):
        return lax.rem(c + step, nc)

    @pl.when(t < nt - 1)
    def _():
        for k in range(nc):
            pl.semaphore_signal(barrier, inc=1, device_id={"tm": t + 1, "cell": k}, device_id_type=MESH)

    for step in range(1, nc):
        pl.semaphore_signal(barrier, inc=1, device_id={"tm": t, "cell": peer(step)}, device_id_type=MESH)

    nsrc = counts[t]
    ntgt = counts[t + 1]
    mine = nsrc - c * n
    live = lax.broadcasted_iota(jnp.int32, (1, n), 1) < mine
    x = jnp.where(live, points[0], 0.0)
    sqx = jnp.sum(x * x, axis=0, keepdims=True)
    growth = jnp.zeros((1, n), f32)
    for k in range(rates.shape[1]):
        growth = jnp.where(bins[...] == k, rates[0, k], growth)
    stats[c] = lane_totals(jnp.concatenate([x, sqx, jnp.where(live, growth, 0.0)], axis=0))
    x1, x2, x3 = splits(jnp.concatenate([-2.0 * x, sqx, jnp.ones((1, n), f32)], axis=0))
    stacked = jnp.concatenate([x1, x1, x2, x2, x1, x3], axis=0)
    lhs[...] = stacked.T

    @pl.when(t == 0)
    def _():
        pl.semaphore_wait(barrier, nc - 1)

    @pl.when(t > 0)
    def _():
        pl.semaphore_wait(barrier, 2 * nc - 1)

    def stat_copy(step, slot):
        return pltpu.make_async_remote_copy(
            stats.at[slot], stats.at[slot], st_send.at[step], st_recv.at[slot],
            device_id={"tm": t, "cell": peer(step)}, device_id_type=MESH)

    def tgt_copy(step):
        return pltpu.make_async_remote_copy(
            points.at[0], tgt.at[c], tgt_send.at[step], tgt_recv.at[c],
            device_id={"tm": t - 1, "cell": peer(step)}, device_id_type=MESH)

    def last_copy(step):
        return pltpu.make_async_remote_copy(
            last, tgt.at[c], last_send.at[step], tgt_recv.at[c],
            device_id={"tm": t, "cell": peer(step)}, device_id_type=MESH)

    for step in range(1, nc):
        stat_copy(step, c).start()

    @pl.when(t > 0)
    def _():
        for step in range(nc):
            tgt_copy(step).start()

    @pl.when(t == nt - 1)
    def _():
        for step in range(1, nc):
            last_copy(step).start()
        pltpu.make_async_copy(last, tgt.at[c], tgt_recv.at[c]).start()

    for step in range(1, nc):
        stat_copy(step, peer(step)).wait_recv()
    source = tree(jnp.add, [stats[k] for k in range(nc)])
    lane = lax.broadcasted_iota(jnp.int32, (1, LANE), 1)

    def pick(row, index):
        return jnp.sum(jnp.where(lane == index, row, 0.0), axis=1, keepdims=True)

    nsrc_f = nsrc.astype(f32)
    ntgt_f = ntgt.astype(f32)
    gbar = pick(source, pc + 1) / nsrc_f
    level[...] = (jnp.log(growth) - jnp.log(gbar)) * LOG2E

    colpot[...] = jnp.zeros_like(colpot)
    stats[nc] = jnp.zeros((1, LANE), f32)

    def take(step):
        k = peer(step)
        pltpu.make_async_copy(tgt.at[k], tgt.at[k], tgt_recv.at[k]).wait()
        ok = lax.broadcasted_iota(jnp.int32, (1, n), 1) < ntgt - k * n
        y = jnp.where(ok, tgt[k], 0.0)
        sqy = jnp.sum(y * y, axis=0, keepdims=True)
        one = jnp.ones((1, n), f32)
        stats[nc] += lane_totals(jnp.concatenate([y, sqy, jnp.zeros((1, n), f32)], axis=0))
        y1, y2, y3 = splits(jnp.concatenate([y, one, sqy], axis=0))
        rhs = jnp.concatenate([y1, y2, y1, y2, y3, y1], axis=0)
        cols = pl.ds(pl.multiple_of(k * n, LANE), n)
        for rb in range(n // LANE):
            got = jnp.dot(lhs[rb * LANE : (rb + 1) * LANE], rhs, preferred_element_type=f32)
            cost[rb * (LANE // SUB) : (rb + 1) * (LANE // SUB), :, cols] = got.reshape(LANE // SUB, SUB, n)
        dead = jnp.where(ok, 0.0, NEG)
        for b in range(n // LANE):
            colpot[k * (n // LANE) + b] = jnp.broadcast_to(dead[:, b * LANE : (b + 1) * LANE], (SUB, LANE))

    each(nc, take)
    target = stats[nc]
    both = jnp.sum(jnp.where(lane < pc, source * target, 0.0), axis=1, keepdims=True)
    total = ntgt_f * pick(source, pc) + nsrc_f * pick(target, pc) - 2.0 * both
    cbar = total / (nsrc_f * ntgt_f)
    scale = jnp.broadcast_to(-UNIT / cbar, (SUB, LANE))

    half = blocks // HALVES
    per = LANE // SUB

    def rows_part(r, h, first):
        scores = []
        for j in range(h * half, (h + 1) * half):
            piece = cost[r, :, j * LANE : (j + 1) * LANE]
            if first:
                piece = piece * scale
                cost[r, :, j * LANE : (j + 1) * LANE] = piece
            scores.append(piece + colpot[j])
        top = tree(jnp.maximum, scores)
        if h > 0:
            before = row_max[r]
            top = jnp.maximum(top, before)
        add = tree(jnp.add, [jnp.exp2(s - top) for s in scores])
        if h > 0:
            add += row_sum[r] * jnp.exp2(before - top)
        row_max[r] = top
        row_sum[r] = add

    def rows_end(k, final):
        rows = slice(k * per, (k + 1) * per)
        cols = slice(k * LANE, (k + 1) * LANE)
        tops = row_max[rows].reshape(LANE, LANE).T
        adds = row_sum[rows].reshape(LANE, LANE).T
        top = jnp.max(tops, axis=0, keepdims=True)
        lse = top + jnp.log(jnp.sum(adds * jnp.exp2(tops - top), axis=0, keepdims=True)) * LOG2E
        ok = lane + k * LANE < mine
        if final:
            mout[:, cols] = jnp.where(ok, jnp.exp2(fpot[:, cols] + lse), 0.0)
        else:
            value = jnp.where(ok, FI * (level[:, cols] - lse), NEG)
            fpot[:, cols] = value
            pot[rows] = jnp.broadcast_to(value, (LANE, LANE)).T.reshape(per, SUB, LANE)

    def rows_open(h, first):
        @pl.loop(0, tiles // GROUP)
        def _(i):
            for u in range(GROUP):
                rows_part(i * GROUP + u, h, first)

    def rows_close(h, first, final):
        rows_open(h, first)
        for k in range(n // LANE):
            rows_end(k, final)

    def cols_part(it, h):
        @pl.loop(0, half // WIDE)
        def _(i):
            at = [pl.multiple_of((h * half + i * WIDE + b) * LANE, LANE) for b in range(WIDE)]
            tops = [[None, None] for _ in at]
            for r in range(tiles):
                base = pot[r]
                for b in range(WIDE):
                    s = base + cost[r, :, pl.ds(at[b], LANE)]
                    tops[b][r % 2] = s if r < 2 else jnp.maximum(tops[b][r % 2], s)
            top = [jnp.maximum(*pair) for pair in tops]
            sums = [[None, None] for _ in at]
            for r in range(tiles):
                base = pot[r]
                for b in range(WIDE):
                    e = jnp.exp2(base + cost[r, :, pl.ds(at[b], LANE)] - top[b])
                    sums[b][r % 2] = e if r < 2 else sums[b][r % 2] + e
            for b in range(WIDE):
                most = jnp.max(top[b], axis=0, keepdims=True)
                add = (sums[b][0] + sums[b][1]) * jnp.exp2(top[b] - most)
                lse = most + jnp.log(jnp.sum(add, axis=0, keepdims=True)) * LOG2E
                parts[it, c, h, pl.ds(i * WIDE + b, 1)] = lse

    def part_copy(it, step, slot, h):
        return pltpu.make_async_remote_copy(
            parts.at[it, slot, h], parts.at[it, slot, h], p_send.at[it, step, h], p_recv.at[it, slot, h],
            device_id={"tm": t, "cell": peer(step)}, device_id_type=MESH)

    cell_at = (lax.broadcasted_iota(jnp.int32, (half, LANE), 0) * LANE
               + lax.broadcasted_iota(jnp.int32, (half, LANE), 1))

    def joined(it, h):
        for step in range(1, nc):
            part_copy(it, step, peer(step), h).wait_recv()
        pieces = [parts[it, k, h] for k in range(nc)]
        top = tree(jnp.maximum, pieces)
        add = tree(jnp.add, [jnp.exp2(p - top) for p in pieces])
        ok = cell_at < ntgt - h * half * LANE
        hpot = jnp.where(ok, -FJ * (top + jnp.log(add) * LOG2E), NEG)
        for j in range(half):
            colpot[h * half + j] = jnp.broadcast_to(hpot[j : j + 1], (SUB, LANE))

    def one(it, final):
        for h in range(HALVES):
            cols_part(it, h)
            for step in range(1, nc):
                part_copy(it, step, c, h).start()
        joined(it, 0)
        rows_open(0, False)
        joined(it, 1)
        rows_close(1, False, final)

    rows_open(0, True)
    rows_close(1, True, False)

    @pl.loop(0, ITERS - 1)
    def _(it):
        one(it, False)

    one(ITERS - 1, True)
    for k in range(n // LANE):
        cols = slice(k * LANE, (k + 1) * LANE)
        fout[:, cols] = jnp.where(lane + k * LANE < mine, fpot[:, cols] * (1.0 / UNIT), 0.0)
        j = c * (n // LANE) + k
        good = lane + j * LANE < ntgt
        hout[:, cols] = jnp.where(good, colpot[j][0:1] * (1.0 / UNIT), 0.0)

    for step in range(1, nc):
        stat_copy(step, c).wait_send()
        for it in range(ITERS):
            for h in range(HALVES):
                part_copy(it, step, c, h).wait_send()

    @pl.when(t > 0)
    def _():
        for step in range(nc):
            tgt_copy(step).wait_send()

    @pl.when(t == nt - 1)
    def _():
        for step in range(1, nc):
            last_copy(step).wait_send()


def local(points, last_points, counts, bins, rates):
    nt = lax.axis_size("tm")
    nc = lax.axis_size("cell")
    pc, n = last_points.shape
    cells = nc * n
    f32 = jnp.float32
    vmem = pl.BlockSpec(memory_space=pltpu.VMEM)
    smem = pl.BlockSpec(memory_space=pltpu.SMEM)
    row = jax.ShapeDtypeStruct((1, n), f32)
    tile = pltpu.VMEM((n // SUB, SUB, LANE), f32)
    dma = pltpu.SemaphoreType.DMA
    return pl.pallas_call(
        functools.partial(kernel, nt, nc),
        out_shape=(row, row, row),
        in_specs=[vmem, vmem, smem, vmem, smem],
        out_specs=(vmem, vmem, vmem),
        scratch_shapes=[
            pltpu.VMEM((n // SUB, SUB, cells), f32),
            pltpu.VMEM((nc, pc, n), f32),
            pltpu.VMEM((nc + 1, 1, LANE), f32),
            pltpu.VMEM((ITERS, nc, HALVES, cells // LANE // HALVES, LANE), f32),
            pltpu.VMEM((n, 6 * (pc + 2)), jnp.bfloat16),
            tile, tile, tile,
            pltpu.VMEM((1, n), f32), pltpu.VMEM((1, n), f32),
            pltpu.VMEM((cells // LANE, SUB, LANE), f32),
            dma((nc,)), dma((nc,)), dma((nc,)), dma((nc,)), dma((nc,)),
            dma((ITERS, nc, HALVES)), dma((ITERS, nc, HALVES)),
        ],
        compiler_params=pltpu.CompilerParams(
            collective_id=0, has_side_effects=True, vmem_limit_bytes=48 * 1024 * 1024
        ),
        name="coupling",
    )(points, last_points, counts, bins, rates)


def solution(mesh):
    return jax.shard_map(
        local,
        mesh=mesh,
        in_specs=(P("tm", None, "cell"), P(None, "cell"), P(), P("tm", "cell"), P("tm", None)),
        out_specs=(P("tm", "cell"), P("tm", "cell"), P("tm", "cell")),
        check_vma=False,
    )
```

```python
import functools
import math

import jax
import jax.numpy as jnp
from jax import lax
from jax.experimental import pallas as pl
from jax.experimental.pallas import tpu as pltpu
from jax.sharding import PartitionSpec as P

ITERS = 4

EPS = 0.05
FI = 1.0 / 1.05
FJ = 50.0 / 50.05
NEG = -1e30
LOG2E = math.log2(math.e)
UNIT = LOG2E / EPS

LANE = 128
HALVES = 2
GROUP = 16
WIDE = 4
SUB = 8
MESH = pl.DeviceIdType.MESH


def each(count, body):
    if count <= 4:
        for item in range(count):
            body(item)
    else:
        pl.loop(0, count)(body)


def tree(join, parts):
    while len(parts) > 1:
        parts = [join(*parts[i : i + 2]) if i + 1 < len(parts) else parts[i] for i in range(0, len(parts), 2)]
    return parts[0]


def splits(value):
    first = value.astype(jnp.bfloat16)
    rest = value - first.astype(jnp.float32)
    second = rest.astype(jnp.bfloat16)
    third = (rest - second.astype(jnp.float32)).astype(jnp.bfloat16)
    return first, second, third


def lane_totals(rows):
    part = tree(jnp.add, [rows[:, i : i + LANE] for i in range(0, rows.shape[1], LANE)])
    whole = jnp.concatenate([part, jnp.zeros((LANE - part.shape[0], LANE), jnp.float32)], axis=0)
    return jnp.sum(whole.T, axis=0, keepdims=True)


def kernel(nt, nc, points, last, counts, bins, rates, fout, hout, mout,
           cost, tgt, stats, sums, parts, lhs, pot, row_max, row_sum, level, fpot, colpot,
           tgt_send, last_send, tgt_recv, st_send, st_recv, p_send, p_recv):
    t = lax.axis_index("tm")
    c = lax.axis_index("cell")
    pc, n = tgt.shape[1:]
    cells = nc * n
    tiles = n // SUB
    blocks = cells // LANE
    f32 = jnp.float32

    barrier = pltpu.get_barrier_semaphore()

    def peer(step):
        return lax.rem(c + step, nc)

    @pl.when(t < nt - 1)
    def _():
        for k in range(nc):
            pl.semaphore_signal(barrier, inc=1, device_id={"tm": t + 1, "cell": k}, device_id_type=MESH)

    for step in range(1, nc):
        pl.semaphore_signal(barrier, inc=1, device_id={"tm": t, "cell": peer(step)}, device_id_type=MESH)

    nsrc = counts[t]
    ntgt = counts[t + 1]
    mine = nsrc - c * n
    live = lax.broadcasted_iota(jnp.int32, (1, n), 1) < mine
    x = jnp.where(live, points[0], 0.0)
    sqx = jnp.sum(x * x, axis=0, keepdims=True)
    growth = jnp.zeros((1, n), f32)
    for k in range(rates.shape[1]):
        growth = jnp.where(bins[...] == k, rates[0, k], growth)
    stats[c] = lane_totals(jnp.concatenate([x, sqx, jnp.where(live, growth, 0.0)], axis=0))

    @pl.when(t == 0)
    def _():
        pl.semaphore_wait(barrier, nc - 1)

    @pl.when(t > 0)
    def _():
        pl.semaphore_wait(barrier, 2 * nc - 1)

    def stat_copy(step, slot):
        return pltpu.make_async_remote_copy(
            stats.at[slot], stats.at[slot], st_send.at[step], st_recv.at[slot],
            device_id={"tm": t, "cell": peer(step)}, device_id_type=MESH)

    def tgt_copy(step):
        return pltpu.make_async_remote_copy(
            points.at[0], tgt.at[c], tgt_send.at[step], tgt_recv.at[c],
            device_id={"tm": t - 1, "cell": peer(step)}, device_id_type=MESH)

    def last_copy(step):
        return pltpu.make_async_remote_copy(
            last, tgt.at[c], last_send.at[step], tgt_recv.at[c],
            device_id={"tm": t, "cell": peer(step)}, device_id_type=MESH)

    for step in range(1, nc):
        stat_copy(step, c).start()

    @pl.when(t > 0)
    def _():
        for step in range(nc):
            tgt_copy(step).start()

    @pl.when(t == nt - 1)
    def _():
        for step in range(1, nc):
            last_copy(step).start()
        pltpu.make_async_copy(last, tgt.at[c], tgt_recv.at[c]).start()

    x1, x2, x3 = splits(jnp.concatenate([-2.0 * x, sqx, jnp.ones((1, n), f32)], axis=0))
    stacked = jnp.concatenate([x1, x1, x2, x2, x1, x3], axis=0)
    lhs[...] = stacked.T

    for step in range(1, nc):
        stat_copy(step, peer(step)).wait_recv()
    source = tree(jnp.add, [stats[k] for k in range(nc)])
    lane = lax.broadcasted_iota(jnp.int32, (1, LANE), 1)

    def pick(row, index):
        return jnp.sum(jnp.where(lane == index, row, 0.0), axis=1, keepdims=True)

    nsrc_f = nsrc.astype(f32)
    ntgt_f = ntgt.astype(f32)
    gbar = pick(source, pc + 1) / nsrc_f
    level[...] = (jnp.log(growth) - jnp.log(gbar)) * LOG2E

    colpot[...] = jnp.zeros_like(colpot)
    sums[...] = jnp.zeros_like(sums)

    def take(step):
        k = peer(step)
        pltpu.make_async_copy(tgt.at[k], tgt.at[k], tgt_recv.at[k]).wait()
        ok = lax.broadcasted_iota(jnp.int32, (1, n), 1) < ntgt - k * n
        y = jnp.where(ok, tgt[k], 0.0)
        sqy = jnp.sum(y * y, axis=0, keepdims=True)
        one = jnp.ones((1, n), f32)
        both = jnp.concatenate([y, sqy, jnp.zeros((1, n), f32)], axis=0)
        sums[...] += tree(jnp.add, [both[:, i : i + LANE] for i in range(0, n, LANE)])
        y1, y2, y3 = splits(jnp.concatenate([y, one, sqy], axis=0))
        rhs = jnp.concatenate([y1, y2, y1, y2, y3, y1], axis=0)
        cols = pl.ds(pl.multiple_of(k * n, LANE), n)
        got = jnp.dot(lhs[...], rhs, preferred_element_type=f32)
        cost[:, :, cols] = got.reshape(tiles, SUB, n)
        dead = jnp.where(ok, 0.0, NEG)
        for b in range(n // LANE):
            colpot[k * (n // LANE) + b] = jnp.broadcast_to(dead[:, b * LANE : (b + 1) * LANE], (SUB, LANE))

    each(nc, take)
    target = lane_totals(sums[...])
    both = jnp.sum(jnp.where(lane < pc, source * target, 0.0), axis=1, keepdims=True)
    total = ntgt_f * pick(source, pc) + nsrc_f * pick(target, pc) - 2.0 * both
    cbar = total / (nsrc_f * ntgt_f)
    scale = jnp.broadcast_to(-UNIT / cbar, (SUB, LANE))

    half = blocks // HALVES
    per = LANE // SUB

    def rows_part(r, h, first):
        scores = []
        for j in range(h * half, (h + 1) * half):
            piece = cost[r, :, j * LANE : (j + 1) * LANE]
            if first:
                piece = piece * scale
                cost[r, :, j * LANE : (j + 1) * LANE] = piece
            scores.append(piece + colpot[j])
        top = tree(jnp.maximum, scores)
        if h > 0:
            before = row_max[r]
            top = jnp.maximum(top, before)
        add = tree(jnp.add, [jnp.exp2(s - top) for s in scores])
        if h > 0:
            add += row_sum[r] * jnp.exp2(before - top)
        row_max[r] = top
        row_sum[r] = add

    def rows_end(k, final):
        rows = slice(k * per, (k + 1) * per)
        cols = slice(k * LANE, (k + 1) * LANE)
        tops = row_max[rows].reshape(LANE, LANE).T
        adds = row_sum[rows].reshape(LANE, LANE).T
        top = jnp.max(tops, axis=0, keepdims=True)
        lse = top + jnp.log(jnp.sum(adds * jnp.exp2(tops - top), axis=0, keepdims=True)) * LOG2E
        ok = lane + k * LANE < mine
        if final:
            mout[:, cols] = jnp.where(ok, jnp.exp2(fpot[:, cols] + lse), 0.0)
        else:
            value = jnp.where(ok, FI * (level[:, cols] - lse), NEG)
            fpot[:, cols] = value
            pot[rows] = jnp.broadcast_to(value, (LANE, LANE)).T.reshape(per, SUB, LANE)

    def rows_open(h, first):
        @pl.loop(0, tiles // GROUP)
        def _(i):
            for u in range(GROUP):
                rows_part(i * GROUP + u, h, first)

    def rows_close(h, first, final):
        rows_open(h, first)
        for k in range(n // LANE):
            rows_end(k, final)

    def cols_part(it, h):
        @pl.loop(0, half // WIDE)
        def _(i):
            at = [pl.multiple_of((h * half + i * WIDE + b) * LANE, LANE) for b in range(WIDE)]
            tops = [[None, None] for _ in at]
            for r in range(tiles):
                base = pot[r]
                for b in range(WIDE):
                    s = base + cost[r, :, pl.ds(at[b], LANE)]
                    tops[b][r % 2] = s if r < 2 else jnp.maximum(tops[b][r % 2], s)
            top = [jnp.maximum(*pair) for pair in tops]
            adds = [[None, None] for _ in at]
            for r in range(tiles):
                base = pot[r]
                for b in range(WIDE):
                    e = jnp.exp2(base + cost[r, :, pl.ds(at[b], LANE)] - top[b])
                    adds[b][r % 2] = e if r < 2 else adds[b][r % 2] + e
            for b in range(WIDE):
                most = jnp.max(top[b], axis=0, keepdims=True)
                add = (adds[b][0] + adds[b][1]) * jnp.exp2(top[b] - most)
                lse = most + jnp.log(jnp.sum(add, axis=0, keepdims=True)) * LOG2E
                parts[it, c, h, pl.ds(i * WIDE + b, 1)] = lse

    def part_copy(it, step, slot, h):
        return pltpu.make_async_remote_copy(
            parts.at[it, slot, h], parts.at[it, slot, h], p_send.at[it, step, h], p_recv.at[it, slot, h],
            device_id={"tm": t, "cell": peer(step)}, device_id_type=MESH)

    cell_at = (lax.broadcasted_iota(jnp.int32, (half, LANE), 0) * LANE
               + lax.broadcasted_iota(jnp.int32, (half, LANE), 1))

    def joined(it, h):
        for step in range(1, nc):
            part_copy(it, step, peer(step), h).wait_recv()
        pieces = [parts[it, k, h] for k in range(nc)]
        top = tree(jnp.maximum, pieces)
        add = tree(jnp.add, [jnp.exp2(p - top) for p in pieces])
        ok = cell_at < ntgt - h * half * LANE
        hpot = jnp.where(ok, -FJ * (top + jnp.log(add) * LOG2E), NEG)
        for j in range(half):
            colpot[h * half + j] = jnp.broadcast_to(hpot[j : j + 1], (SUB, LANE))

    def one(it, final):
        for h in range(HALVES):
            cols_part(it, h)
            for step in range(1, nc):
                part_copy(it, step, c, h).start()
        joined(it, 0)
        rows_open(0, False)
        joined(it, 1)
        rows_close(1, False, final)

    rows_open(0, True)
    rows_close(1, True, False)

    @pl.loop(0, ITERS - 1)
    def _(it):
        one(it, False)

    one(ITERS - 1, True)
    for k in range(n // LANE):
        cols = slice(k * LANE, (k + 1) * LANE)
        fout[:, cols] = jnp.where(lane + k * LANE < mine, fpot[:, cols] * (1.0 / UNIT), 0.0)
        j = c * (n // LANE) + k
        good = lane + j * LANE < ntgt
        hout[:, cols] = jnp.where(good, colpot[j][0:1] * (1.0 / UNIT), 0.0)

    for step in range(1, nc):
        stat_copy(step, c).wait_send()
        for it in range(ITERS):
            for h in range(HALVES):
                part_copy(it, step, c, h).wait_send()

    @pl.when(t > 0)
    def _():
        for step in range(nc):
            tgt_copy(step).wait_send()

    @pl.when(t == nt - 1)
    def _():
        for step in range(1, nc):
            last_copy(step).wait_send()


def local(points, last_points, counts, bins, rates):
    nt = lax.axis_size("tm")
    nc = lax.axis_size("cell")
    pc, n = last_points.shape
    cells = nc * n
    f32 = jnp.float32
    vmem = pl.BlockSpec(memory_space=pltpu.VMEM)
    smem = pl.BlockSpec(memory_space=pltpu.SMEM)
    row = jax.ShapeDtypeStruct((1, n), f32)
    tile = pltpu.VMEM((n // SUB, SUB, LANE), f32)
    dma = pltpu.SemaphoreType.DMA
    return pl.pallas_call(
        functools.partial(kernel, nt, nc),
        out_shape=(row, row, row),
        in_specs=[vmem, vmem, smem, vmem, smem],
        out_specs=(vmem, vmem, vmem),
        scratch_shapes=[
            pltpu.VMEM((n // SUB, SUB, cells), f32),
            pltpu.VMEM((nc, pc, n), f32),
            pltpu.VMEM((nc, 1, LANE), f32),
            pltpu.VMEM((pc + 2, LANE), f32),
            pltpu.VMEM((ITERS, nc, HALVES, cells // LANE // HALVES, LANE), f32),
            pltpu.VMEM((n, 6 * (pc + 2)), jnp.bfloat16),
            tile, tile, tile,
            pltpu.VMEM((1, n), f32), pltpu.VMEM((1, n), f32),
            pltpu.VMEM((cells // LANE, SUB, LANE), f32),
            dma((nc,)), dma((nc,)), dma((nc,)), dma((nc,)), dma((nc,)),
            dma((ITERS, nc, HALVES)), dma((ITERS, nc, HALVES)),
        ],
        compiler_params=pltpu.CompilerParams(
            collective_id=0, has_side_effects=True, vmem_limit_bytes=48 * 1024 * 1024
        ),
        name="coupling",
    )(points, last_points, counts, bins, rates)


def solution(mesh):
    return jax.shard_map(
        local,
        mesh=mesh,
        in_specs=(P("tm", None, "cell"), P(None, "cell"), P(), P("tm", "cell"), P("tm", None)),
        out_specs=(P("tm", "cell"), P("tm", "cell"), P("tm", "cell")),
        check_vma=False,
    )
```

```python
import functools
import math

import jax
import jax.numpy as jnp
from jax import lax
from jax.experimental import pallas as pl
from jax.experimental.pallas import tpu as pltpu
from jax.sharding import PartitionSpec as P

ITERS = 4

EPS = 0.05
FI = 1.0 / 1.05
FJ = 50.0 / 50.05
NEG = -1e30
LOG2E = math.log2(math.e)
UNIT = LOG2E / EPS

LANE = 128
HALVES = 2
GROUP = 32
WIDE = 8
SUB = 8
MESH = pl.DeviceIdType.MESH


def each(count, body):
    if count <= 4:
        for item in range(count):
            body(item)
    else:
        pl.loop(0, count)(body)


def tree(join, parts):
    while len(parts) > 1:
        parts = [join(*parts[i : i + 2]) if i + 1 < len(parts) else parts[i] for i in range(0, len(parts), 2)]
    return parts[0]


def splits(value):
    first = value.astype(jnp.bfloat16)
    rest = value - first.astype(jnp.float32)
    second = rest.astype(jnp.bfloat16)
    third = (rest - second.astype(jnp.float32)).astype(jnp.bfloat16)
    return first, second, third


def lane_totals(rows):
    part = tree(jnp.add, [rows[:, i : i + LANE] for i in range(0, rows.shape[1], LANE)])
    whole = jnp.concatenate([part, jnp.zeros((LANE - part.shape[0], LANE), jnp.float32)], axis=0)
    return jnp.sum(whole.T, axis=0, keepdims=True)


def kernel(nt, nc, points, last, counts, bins, rates, fout, hout, mout,
           cost, tgt, stats, sums, parts, lhs, pot, row_max, row_sum, level, fpot, colpot,
           tgt_send, last_send, tgt_recv, st_send, st_recv, p_send, p_recv):
    t = lax.axis_index("tm")
    c = lax.axis_index("cell")
    pc, n = tgt.shape[1:]
    cells = nc * n
    tiles = n // SUB
    blocks = cells // LANE
    f32 = jnp.float32

    barrier = pltpu.get_barrier_semaphore()

    def peer(step):
        return lax.rem(c + step, nc)

    @pl.when(t < nt - 1)
    def _():
        for k in range(nc):
            pl.semaphore_signal(barrier, inc=1, device_id={"tm": t + 1, "cell": k}, device_id_type=MESH)

    for step in range(1, nc):
        pl.semaphore_signal(barrier, inc=1, device_id={"tm": t, "cell": peer(step)}, device_id_type=MESH)

    nsrc = counts[t]
    ntgt = counts[t + 1]
    mine = nsrc - c * n
    live = lax.broadcasted_iota(jnp.int32, (1, n), 1) < mine
    x = jnp.where(live, points[0], 0.0)
    sqx = jnp.sum(x * x, axis=0, keepdims=True)
    growth = jnp.zeros((1, n), f32)
    for k in range(rates.shape[1]):
        growth = jnp.where(bins[...] == k, rates[0, k], growth)
    stats[c] = lane_totals(jnp.concatenate([x, sqx, jnp.where(live, growth, 0.0)], axis=0))

    @pl.when(t == 0)
    def _():
        pl.semaphore_wait(barrier, nc - 1)

    @pl.when(t > 0)
    def _():
        pl.semaphore_wait(barrier, 2 * nc - 1)

    def stat_copy(step, slot):
        return pltpu.make_async_remote_copy(
            stats.at[slot], stats.at[slot], st_send.at[step], st_recv.at[slot],
            device_id={"tm": t, "cell": peer(step)}, device_id_type=MESH)

    def tgt_copy(step):
        return pltpu.make_async_remote_copy(
            points.at[0], tgt.at[c], tgt_send.at[step], tgt_recv.at[c],
            device_id={"tm": t - 1, "cell": peer(step)}, device_id_type=MESH)

    def last_copy(step):
        return pltpu.make_async_remote_copy(
            last, tgt.at[c], last_send.at[step], tgt_recv.at[c],
            device_id={"tm": t, "cell": peer(step)}, device_id_type=MESH)

    for step in range(1, nc):
        stat_copy(step, c).start()

    @pl.when(t > 0)
    def _():
        for step in range(nc):
            tgt_copy(step).start()

    @pl.when(t == nt - 1)
    def _():
        for step in range(1, nc):
            last_copy(step).start()
        pltpu.make_async_copy(last, tgt.at[c], tgt_recv.at[c]).start()

    x1, x2, x3 = splits(jnp.concatenate([-2.0 * x, sqx, jnp.ones((1, n), f32)], axis=0))
    stacked = jnp.concatenate([x1, x1, x2, x2, x1, x3], axis=0)
    lhs[...] = stacked.T

    for step in range(1, nc):
        stat_copy(step, peer(step)).wait_recv()
    source = tree(jnp.add, [stats[k] for k in range(nc)])
    lane = lax.broadcasted_iota(jnp.int32, (1, LANE), 1)

    def pick(row, index):
        return jnp.sum(jnp.where(lane == index, row, 0.0), axis=1, keepdims=True)

    nsrc_f = nsrc.astype(f32)
    ntgt_f = ntgt.astype(f32)
    gbar = pick(source, pc + 1) / nsrc_f
    level[...] = (jnp.log(growth) - jnp.log(gbar)) * LOG2E

    colpot[...] = jnp.zeros_like(colpot)
    sums[...] = jnp.zeros_like(sums)

    def take(step):
        k = peer(step)
        pltpu.make_async_copy(tgt.at[k], tgt.at[k], tgt_recv.at[k]).wait()
        ok = lax.broadcasted_iota(jnp.int32, (1, n), 1) < ntgt - k * n
        y = jnp.where(ok, tgt[k], 0.0)
        sqy = jnp.sum(y * y, axis=0, keepdims=True)
        one = jnp.ones((1, n), f32)
        both = jnp.concatenate([y, sqy, jnp.zeros((1, n), f32)], axis=0)
        sums[...] += tree(jnp.add, [both[:, i : i + LANE] for i in range(0, n, LANE)])
        y1, y2, y3 = splits(jnp.concatenate([y, one, sqy], axis=0))
        rhs = jnp.concatenate([y1, y2, y1, y2, y3, y1], axis=0)
        cols = pl.ds(pl.multiple_of(k * n, LANE), n)
        got = jnp.dot(lhs[...], rhs, preferred_element_type=f32)
        cost[:, :, cols] = got.reshape(tiles, SUB, n)
        dead = jnp.where(ok, 0.0, NEG)
        for b in range(n // LANE):
            colpot[k * (n // LANE) + b] = jnp.broadcast_to(dead[:, b * LANE : (b + 1) * LANE], (SUB, LANE))

    each(nc, take)
    target = lane_totals(sums[...])
    both = jnp.sum(jnp.where(lane < pc, source * target, 0.0), axis=1, keepdims=True)
    total = ntgt_f * pick(source, pc) + nsrc_f * pick(target, pc) - 2.0 * both
    cbar = total / (nsrc_f * ntgt_f)
    scale = jnp.broadcast_to(-UNIT / cbar, (SUB, LANE))

    half = blocks // HALVES
    per = LANE // SUB

    def rows_part(r, h, first):
        scores = []
        for j in range(h * half, (h + 1) * half):
            piece = cost[r, :, j * LANE : (j + 1) * LANE]
            if first:
                piece = piece * scale
                cost[r, :, j * LANE : (j + 1) * LANE] = piece
            scores.append(piece + colpot[j])
        top = tree(jnp.maximum, scores)
        if h > 0:
            before = row_max[r]
            top = jnp.maximum(top, before)
        add = tree(jnp.add, [jnp.exp2(s - top) for s in scores])
        if h > 0:
            add += row_sum[r] * jnp.exp2(before - top)
        row_max[r] = top
        row_sum[r] = add

    def rows_end(k, final):
        rows = slice(k * per, (k + 1) * per)
        cols = slice(k * LANE, (k + 1) * LANE)
        tops = row_max[rows].reshape(LANE, LANE).T
        adds = row_sum[rows].reshape(LANE, LANE).T
        top = jnp.max(tops, axis=0, keepdims=True)
        lse = top + jnp.log(jnp.sum(adds * jnp.exp2(tops - top), axis=0, keepdims=True)) * LOG2E
        ok = lane + k * LANE < mine
        if final:
            mout[:, cols] = jnp.where(ok, jnp.exp2(fpot[:, cols] + lse), 0.0)
        else:
            value = jnp.where(ok, FI * (level[:, cols] - lse), NEG)
            fpot[:, cols] = value
            pot[rows] = jnp.broadcast_to(value, (LANE, LANE)).T.reshape(per, SUB, LANE)

    def rows_open(h, first):
        @pl.loop(0, tiles // GROUP)
        def _(i):
            for u in range(GROUP):
                rows_part(i * GROUP + u, h, first)

    def rows_close(h, first, final):
        rows_open(h, first)
        for k in range(n // LANE):
            rows_end(k, final)

    def cols_part(it, h):
        @pl.loop(0, half // WIDE)
        def _(i):
            at = [pl.multiple_of((h * half + i * WIDE + b) * LANE, LANE) for b in range(WIDE)]
            tops = [[None, None] for _ in at]
            for r in range(tiles):
                base = pot[r]
                for b in range(WIDE):
                    s = base + cost[r, :, pl.ds(at[b], LANE)]
                    tops[b][r % 2] = s if r < 2 else jnp.maximum(tops[b][r % 2], s)
            top = [jnp.maximum(*pair) for pair in tops]
            adds = [[None, None] for _ in at]
            for r in range(tiles):
                base = pot[r]
                for b in range(WIDE):
                    e = jnp.exp2(base + cost[r, :, pl.ds(at[b], LANE)] - top[b])
                    adds[b][r % 2] = e if r < 2 else adds[b][r % 2] + e
            for b in range(WIDE):
                most = jnp.max(top[b], axis=0, keepdims=True)
                add = (adds[b][0] + adds[b][1]) * jnp.exp2(top[b] - most)
                lse = most + jnp.log(jnp.sum(add, axis=0, keepdims=True)) * LOG2E
                parts[it, c, h, pl.ds(i * WIDE + b, 1)] = lse

    def part_copy(it, step, slot, h):
        return pltpu.make_async_remote_copy(
            parts.at[it, slot, h], parts.at[it, slot, h], p_send.at[it, step, h], p_recv.at[it, slot, h],
            device_id={"tm": t, "cell": peer(step)}, device_id_type=MESH)

    cell_at = (lax.broadcasted_iota(jnp.int32, (half, LANE), 0) * LANE
               + lax.broadcasted_iota(jnp.int32, (half, LANE), 1))

    def joined(it, h):
        for step in range(1, nc):
            part_copy(it, step, peer(step), h).wait_recv()
        pieces = [parts[it, k, h] for k in range(nc)]
        top = tree(jnp.maximum, pieces)
        add = tree(jnp.add, [jnp.exp2(p - top) for p in pieces])
        ok = cell_at < ntgt - h * half * LANE
        hpot = jnp.where(ok, -FJ * (top + jnp.log(add) * LOG2E), NEG)
        for j in range(half):
            colpot[h * half + j] = jnp.broadcast_to(hpot[j : j + 1], (SUB, LANE))

    def one(it, final):
        for h in range(HALVES):
            cols_part(it, h)
            for step in range(1, nc):
                part_copy(it, step, c, h).start()
        joined(it, 0)
        rows_open(0, False)
        joined(it, 1)
        rows_close(1, False, final)

    rows_open(0, True)
    rows_close(1, True, False)

    @pl.loop(0, ITERS - 1)
    def _(it):
        one(it, False)

    one(ITERS - 1, True)
    for k in range(n // LANE):
        cols = slice(k * LANE, (k + 1) * LANE)
        fout[:, cols] = jnp.where(lane + k * LANE < mine, fpot[:, cols] * (1.0 / UNIT), 0.0)
        j = c * (n // LANE) + k
        good = lane + j * LANE < ntgt
        hout[:, cols] = jnp.where(good, colpot[j][0:1] * (1.0 / UNIT), 0.0)

    for step in range(1, nc):
        stat_copy(step, c).wait_send()
        for it in range(ITERS):
            for h in range(HALVES):
                part_copy(it, step, c, h).wait_send()

    @pl.when(t > 0)
    def _():
        for step in range(nc):
            tgt_copy(step).wait_send()

    @pl.when(t == nt - 1)
    def _():
        for step in range(1, nc):
            last_copy(step).wait_send()


def local(points, last_points, counts, bins, rates):
    nt = lax.axis_size("tm")
    nc = lax.axis_size("cell")
    pc, n = last_points.shape
    cells = nc * n
    f32 = jnp.float32
    vmem = pl.BlockSpec(memory_space=pltpu.VMEM)
    smem = pl.BlockSpec(memory_space=pltpu.SMEM)
    row = jax.ShapeDtypeStruct((1, n), f32)
    tile = pltpu.VMEM((n // SUB, SUB, LANE), f32)
    dma = pltpu.SemaphoreType.DMA
    return pl.pallas_call(
        functools.partial(kernel, nt, nc),
        out_shape=(row, row, row),
        in_specs=[vmem, vmem, smem, vmem, smem],
        out_specs=(vmem, vmem, vmem),
        scratch_shapes=[
            pltpu.VMEM((n // SUB, SUB, cells), f32),
            pltpu.VMEM((nc, pc, n), f32),
            pltpu.VMEM((nc, 1, LANE), f32),
            pltpu.VMEM((pc + 2, LANE), f32),
            pltpu.VMEM((ITERS, nc, HALVES, cells // LANE // HALVES, LANE), f32),
            pltpu.VMEM((n, 6 * (pc + 2)), jnp.bfloat16),
            tile, tile, tile,
            pltpu.VMEM((1, n), f32), pltpu.VMEM((1, n), f32),
            pltpu.VMEM((cells // LANE, SUB, LANE), f32),
            dma((nc,)), dma((nc,)), dma((nc,)), dma((nc,)), dma((nc,)),
            dma((ITERS, nc, HALVES)), dma((ITERS, nc, HALVES)),
        ],
        compiler_params=pltpu.CompilerParams(
            collective_id=0, has_side_effects=True, vmem_limit_bytes=48 * 1024 * 1024
        ),
        name="coupling",
    )(points, last_points, counts, bins, rates)


def solution(mesh):
    return jax.shard_map(
        local,
        mesh=mesh,
        in_specs=(P("tm", None, "cell"), P(None, "cell"), P(), P("tm", "cell"), P("tm", None)),
        out_specs=(P("tm", "cell"), P("tm", "cell"), P("tm", "cell")),
        check_vma=False,
    )
```
